32 devices in a mesh: groups: 2 (over x), seq: 16 (over z, y, core).
Axes of the slice: x: 2, y: 2, z: 4, core: 2. Of those that a mesh axis runs over, the one named last changes fastest.
Arguments:
- queries: bfloat16 [4096, 4096], P(('groups', 'seq')), parts along dimension 0, may hold values from -200 to 200
- response_keys: bfloat16 [4096, 512], P(('groups', 'seq')), parts along dimension 0, may hold values from -6 to 6
- response_values: bfloat16 [4096, 512], P(('groups', 'seq')), parts along dimension 0, may hold values from -6 to 6
- prompt_key_rows: bfloat16 [8192, 512], P(('groups', 'seq')), parts along dimension 0, may hold values from -6 to 6
- prompt_value_rows: bfloat16 [8192, 512], P(('groups', 'seq')), parts along dimension 0, may hold values from -6 to 6
- upstream: bfloat16 [4096, 4096], P(('groups', 'seq')), parts along dimension 0, may hold values from -6 to 6
- prompt_len: int32 [8], P('groups'), parts along dimension 0, may hold values from 256 to 1024, as said below
- prompt_owner: int32 [8], P('groups'), parts along dimension 0, may hold values from 0 to 3, as said below
- response_prompt: int32 [64], P(('groups', 'seq')), parts along dimension 0, may hold values from 0 to 3, as said below
- response_len: int32 [64], P(('groups', 'seq')), parts along dimension 0, may hold values from 1 to 64, as said below
Outputs:
- attn_out: bfloat16 [4096, 4096], P(('groups', 'seq')), parts along dimension 0
- grad_queries: bfloat16 [4096, 4096], P(('groups', 'seq')), parts along dimension 0
- grad_resp_keys: bfloat16 [4096, 512], P(('groups', 'seq')), parts along dimension 0
- grad_resp_values: bfloat16 [4096, 512], P(('groups', 'seq')), parts along dimension 0
- grad_prefix_keys: float32 [8192, 512], P(('groups', 'seq')), parts along dimension 0
- grad_prefix_values: float32 [8192, 512], P(('groups', 'seq')), parts along dimension 0
The draws below stay inside these ranges and needn't reach their ends.
There are 2 independent parts, one for each index of `groups`. The reference program is written for one: setup_inputs(seed, part) draws one part's arguments, and reference() takes and returns one part's arrays. A program takes and returns all parts, laid end to end along the dimension named above; each array names one. Nothing has to cross between parts.
Inputs may be any that keep to these rules, and one draw needn't show every extreme that they name: `prompt_len`: some prompt has exactly 1024 tokens. `prompt_owner`: A permutation of the blocks; block b is the devices b * 4 to (b + 1) * 4 - 1, which hold prefix rows b * 1024 to (b + 1) * 1024 - 1. `response_prompt`: the 8 slots of block c (slots c * 8 to (c + 1) * 8 - 1) all hold responses of one prompt, owned by block c or by block c xor 1; blocks c and c xor 1 either both hold their own prompts or hold each other's. So each prompt has 8 responses. `response_len`: some response has exactly 64 tokens.
All inputs are finite; a program needn't handle non-finite values.
Results may differ from the reference program's by a relative error of at most 0.005.
Values may be sent and summed in bfloat16 or wider, within the bound.
A program may use at most 64 MiB of HBM per device.

```python
import math
import jax
import jax.numpy as jnp
from jax import lax

QUERY_HEADS = 32
KEY_VALUE_HEADS = 4
HEAD_WIDTH = 128
GROUP_RESPONSES = 8
RESPONSE_LENGTH = 64
PROMPT_MAXIMUM = 1024
PROMPT_COUNT = 4


def owner_layout(key, part):
    owner_perm = jax.random.permutation(jax.random.fold_in(key, 201), PROMPT_COUNT).astype(jnp.int32)
    pair_count = PROMPT_COUNT // 2
    flipped_pairs = jax.random.randint(jax.random.fold_in(key, 202), (pair_count,), 0, 2)
    kept_flip = jax.random.randint(jax.random.fold_in(key, 203), (), 0, pair_count)
    pair_ids = jnp.arange(pair_count, dtype=jnp.int32)
    flipped_pairs = jnp.where(pair_ids == kept_flip, 1, flipped_pairs).astype(jnp.int32)
    first_host = flipped_pairs[0]
    target = (jnp.asarray(part).astype(jnp.int32) % PROMPT_COUNT).astype(jnp.int32)
    prompt_ids = jnp.arange(PROMPT_COUNT, dtype=jnp.int32)
    holder = jnp.sum(jnp.where(owner_perm == first_host, prompt_ids, 0)).astype(jnp.int32)
    target_owner = jnp.sum(jnp.where(prompt_ids == target, owner_perm, 0)).astype(jnp.int32)
    owner_perm = jnp.where(prompt_ids == target, first_host, jnp.where(prompt_ids == holder, target_owner, owner_perm))
    return (owner_perm.astype(jnp.int32), flipped_pairs)


def draw_prompt_owner(key, part):
    owner_perm, flipped_pairs = owner_layout(key, part)
    return owner_perm


def draw_response_prompt(key, part):
    owner_perm, flipped_pairs = owner_layout(key, part)
    inverse = jnp.argsort(owner_perm).astype(jnp.int32)
    block_ids = jnp.arange(PROMPT_COUNT, dtype=jnp.int32)
    host_block = block_ids + flipped_pairs[block_ids // 2] * (1 - 2 * (block_ids % 2))
    prompt_of_block = inverse[host_block]
    return jnp.repeat(prompt_of_block, GROUP_RESPONSES).astype(jnp.int32)


def draw_prompt_len(key, part):
    key = jax.random.fold_in(key, 21)
    lengths = jax.random.randint(jax.random.fold_in(key, 1), (PROMPT_COUNT,), PROMPT_MAXIMUM // 4, PROMPT_MAXIMUM + 1)
    marked = jax.random.randint(jax.random.fold_in(key, 2), (), 0, PROMPT_COUNT)
    return jnp.where(jnp.arange(PROMPT_COUNT) == marked, PROMPT_MAXIMUM, lengths).astype(jnp.int32)


def draw_response_len(key, part):
    key = jax.random.fold_in(key, 31)
    count_all = PROMPT_COUNT * GROUP_RESPONSES
    lengths = jax.random.randint(jax.random.fold_in(key, 1), (count_all,), 1, RESPONSE_LENGTH + 1)
    marked = jax.random.randint(jax.random.fold_in(key, 2), (), 0, count_all)
    return jnp.where(jnp.arange(count_all) == marked, RESPONSE_LENGTH, lengths).astype(jnp.int32)


def draw_queries(key, part):
    key = jax.random.fold_in(key, 11)
    row_count = PROMPT_COUNT * GROUP_RESPONSES * RESPONSE_LENGTH
    values = jax.random.normal(jax.random.fold_in(key, 1), (row_count, QUERY_HEADS * HEAD_WIDTH), jnp.float32)
    values = jnp.clip(values, -6.0, 6.0)
    return values.astype(jnp.bfloat16)


def shard_levels(stream_key, shape, shards, least, largest):
    gain, own = 1.0, jax.random.fold_in(stream_key, 6)
    for dim, shards_of in shards:
        steps = jnp.exp(jax.random.uniform(jax.random.fold_in(own, dim), (shards_of,), jnp.float32, least / len(shards), largest / len(shards)))
        gain = gain * jnp.repeat(steps, shape[dim] // shards_of).reshape([-1 if axis == dim else 1 for axis in range(len(shape))])
    return gain


def noise(own_key, extent, width, reach, split=(), kind=jnp.bfloat16):
    values = width * jax.random.normal(own_key, extent, jnp.float32)
    if split:
        values = values * shard_levels(own_key, extent, split, -0.22, 0.18)
    return jnp.clip(values, -reach, reach).astype(kind)


def setup_inputs(seed: int = 0, part: int = 0) -> dict:
    streams_of = jax.random.split(jax.random.key(seed), 11)
    own_keys = jax.random.split(jax.random.fold_in(streams_of[10], part), 11)
    return {
        "queries": draw_queries(jax.random.fold_in(jax.random.fold_in(streams_of[10], part), 71), part),
        "response_keys": noise(own_keys[1], (PROMPT_COUNT * GROUP_RESPONSES * RESPONSE_LENGTH, KEY_VALUE_HEADS * HEAD_WIDTH), 1.0, 6.0, ((0, 16),)),
        "response_values": noise(own_keys[2], (PROMPT_COUNT * GROUP_RESPONSES * RESPONSE_LENGTH, KEY_VALUE_HEADS * HEAD_WIDTH), 1.0, 6.0, ((0, 16),)),
        "prompt_key_rows": noise(own_keys[3], (PROMPT_COUNT * PROMPT_MAXIMUM, KEY_VALUE_HEADS * HEAD_WIDTH), 1.0, 6.0, ((0, 16),)),
        "prompt_value_rows": noise(own_keys[4], (PROMPT_COUNT * PROMPT_MAXIMUM, KEY_VALUE_HEADS * HEAD_WIDTH), 1.0, 6.0, ((0, 16),)),
        "upstream": noise(own_keys[5], (PROMPT_COUNT * GROUP_RESPONSES * RESPONSE_LENGTH, QUERY_HEADS * HEAD_WIDTH), 1.0, 6.0, ((0, 16),)),
        "prompt_len": draw_prompt_len(jax.random.fold_in(jax.random.fold_in(streams_of[10], part), 71), part),
        "prompt_owner": draw_prompt_owner(jax.random.fold_in(jax.random.fold_in(streams_of[10], part), 71), part),
        "response_prompt": draw_response_prompt(jax.random.fold_in(jax.random.fold_in(streams_of[10], part), 71), part),
        "response_len": draw_response_len(jax.random.fold_in(jax.random.fold_in(streams_of[10], part), 71), part),
    }


def rounded(values):
    narrow = lax.optimization_barrier(values.astype(jnp.bfloat16))
    return narrow.astype(jnp.float32)

def attend_slot(rows_of_queries, rows_of_keys, rows_of_values, gradient_rows, earlier_keys, earlier_values, pre_len, resp_len):
    heads_per_group = QUERY_HEADS // KEY_VALUE_HEADS
    score_scale = 1.0 / math.sqrt(HEAD_WIDTH)
    complete_query = rows_of_queries.astype(jnp.float32).reshape(RESPONSE_LENGTH, KEY_VALUE_HEADS, heads_per_group, HEAD_WIDTH)
    gradient_complete = gradient_rows.astype(jnp.float32).reshape(RESPONSE_LENGTH, KEY_VALUE_HEADS, heads_per_group, HEAD_WIDTH)
    own_response_keys = rows_of_keys.astype(jnp.float32).reshape(RESPONSE_LENGTH, KEY_VALUE_HEADS, HEAD_WIDTH)
    own_response_values = rows_of_values.astype(jnp.float32).reshape(RESPONSE_LENGTH, KEY_VALUE_HEADS, HEAD_WIDTH)
    common_keys = earlier_keys.astype(jnp.float32).reshape(PROMPT_MAXIMUM, KEY_VALUE_HEADS, HEAD_WIDTH)
    common_values = earlier_values.astype(jnp.float32).reshape(PROMPT_MAXIMUM, KEY_VALUE_HEADS, HEAD_WIDTH)
    positions = jnp.arange(RESPONSE_LENGTH, dtype=jnp.int32)
    live_rows = positions < resp_len
    shared_mask = jnp.arange(PROMPT_MAXIMUM, dtype=jnp.int32) < pre_len
    self_mask = (positions[None, :] <= positions[:, None]) & (positions[None, :] < resp_len)
    shared_scores = jnp.einsum('lgrd,pgd->grlp', complete_query, common_keys) * score_scale
    self_scores = jnp.einsum('igrd,jgd->grij', complete_query, own_response_keys) * score_scale
    shared_scores = jnp.where(shared_mask[None, None, None, :], shared_scores, -jnp.inf)
    self_scores = jnp.where(self_mask[None, None, :, :], self_scores, -jnp.inf)
    row_max = jnp.maximum(lax.optimization_barrier(jnp.max(shared_scores, axis=-1)), lax.optimization_barrier(jnp.max(self_scores, axis=-1)))
    shared_exp = jnp.exp(shared_scores - row_max[..., None])
    self_exp = jnp.exp(self_scores - row_max[..., None])
    row_total = lax.optimization_barrier(jnp.sum(shared_exp, axis=-1)) + lax.optimization_barrier(jnp.sum(self_exp, axis=-1))
    shared_prob = shared_exp / row_total[..., None]
    self_prob = self_exp / row_total[..., None]
    shared_weight = rounded(shared_prob)
    self_weight = rounded(self_prob)
    blended_output = jnp.einsum('grlp,pgd->lgrd', shared_weight, common_values) + jnp.einsum('grij,jgd->igrd', self_weight, own_response_values)
    live_four = live_rows[:, None, None, None]
    blended_output = jnp.where(live_four, blended_output, 0.0)
    gradient_complete = jnp.where(live_four, gradient_complete, 0.0)
    shared_dprob = jnp.einsum('lgrd,pgd->grlp', gradient_complete, common_values)
    self_dprob = jnp.einsum('igrd,jgd->grij', gradient_complete, own_response_values)
    delta_sum = lax.optimization_barrier(jnp.sum(shared_prob * shared_dprob, axis=-1)) + lax.optimization_barrier(jnp.sum(self_prob * self_dprob, axis=-1))
    shared_dscore = rounded(shared_prob * (shared_dprob - delta_sum[..., None]) * score_scale)
    self_dscore = rounded(self_prob * (self_dprob - delta_sum[..., None]) * score_scale)
    query_gradient = jnp.einsum('grlp,pgd->lgrd', shared_dscore, common_keys) + jnp.einsum('grij,jgd->igrd', self_dscore, own_response_keys)
    own_key_gradient = jnp.einsum('grij,igrd->jgd', self_dscore, complete_query)
    own_value_gradient = jnp.einsum('grij,igrd->jgd', self_weight, gradient_complete)
    common_key_gradient = jnp.einsum('grlp,lgrd->pgd', shared_dscore, complete_query)
    common_value_gradient = jnp.einsum('grlp,lgrd->pgd', shared_weight, gradient_complete)
    return (blended_output.reshape(RESPONSE_LENGTH, QUERY_HEADS * HEAD_WIDTH).astype(jnp.bfloat16), query_gradient.reshape(RESPONSE_LENGTH, QUERY_HEADS * HEAD_WIDTH).astype(jnp.bfloat16), own_key_gradient.reshape(RESPONSE_LENGTH, KEY_VALUE_HEADS * HEAD_WIDTH).astype(jnp.bfloat16), own_value_gradient.reshape(RESPONSE_LENGTH, KEY_VALUE_HEADS * HEAD_WIDTH).astype(jnp.bfloat16), common_key_gradient.reshape(PROMPT_MAXIMUM, KEY_VALUE_HEADS * HEAD_WIDTH), common_value_gradient.reshape(PROMPT_MAXIMUM, KEY_VALUE_HEADS * HEAD_WIDTH))

def reference(queries, response_keys, response_values, prompt_key_rows, prompt_value_rows, upstream, prompt_len, prompt_owner, response_prompt, response_len):
    position_count = PROMPT_COUNT * GROUP_RESPONSES
    width_query = QUERY_HEADS * HEAD_WIDTH
    key_width = KEY_VALUE_HEADS * HEAD_WIDTH
    query_slots = queries.reshape(position_count, RESPONSE_LENGTH, width_query)
    upstream_slots = upstream.reshape(position_count, RESPONSE_LENGTH, width_query)
    key_slots = response_keys.reshape(position_count, RESPONSE_LENGTH, key_width)
    value_slots = response_values.reshape(position_count, RESPONSE_LENGTH, key_width)

    def step(totals, slot_item):
        sum_keys, sum_values = totals
        rows_of_queries, rows_of_keys, rows_of_values, gradient_rows, prompt_index, resp_length = slot_item
        owner_block = prompt_owner[prompt_index].astype(jnp.int32)
        pre_length = prompt_len[prompt_index].astype(jnp.int32)
        row_start = (owner_block * PROMPT_MAXIMUM).astype(jnp.int32)
        earlier_keys = lax.dynamic_slice_in_dim(prompt_key_rows, row_start, PROMPT_MAXIMUM, 0)
        earlier_values = lax.dynamic_slice_in_dim(prompt_value_rows, row_start, PROMPT_MAXIMUM, 0)
        results = attend_slot(rows_of_queries, rows_of_keys, rows_of_values, gradient_rows, earlier_keys, earlier_values, pre_length, resp_length)
        current_keys = lax.dynamic_slice_in_dim(sum_keys, row_start, PROMPT_MAXIMUM, 0)
        current_values = lax.dynamic_slice_in_dim(sum_values, row_start, PROMPT_MAXIMUM, 0)
        sum_keys = lax.dynamic_update_slice_in_dim(sum_keys, current_keys + results[4], row_start, 0)
        sum_values = lax.dynamic_update_slice_in_dim(sum_values, current_values + results[5], row_start, 0)
        return ((sum_keys, sum_values), results[:4])
    initial = (jnp.zeros((PROMPT_COUNT * PROMPT_MAXIMUM, key_width), jnp.float32), jnp.zeros((PROMPT_COUNT * PROMPT_MAXIMUM, key_width), jnp.float32))
    (sum_keys, sum_values), outputs = lax.scan(step, initial, (query_slots, key_slots, value_slots, upstream_slots, response_prompt, response_len))
    blended_output, query_gradient, own_key_gradient, own_value_gradient = outputs
    total_rows = position_count * RESPONSE_LENGTH
    return (blended_output.reshape(total_rows, width_query), query_gradient.reshape(total_rows, width_query), own_key_gradient.reshape(total_rows, key_width), own_value_gradient.reshape(total_rows, key_width), sum_keys, sum_values)
```

```python
import math

import jax
import jax.numpy as jnp
from jax import lax
from jax.experimental import pallas as pl
from jax.experimental.pallas import tpu as pltpu
from jax.sharding import PartitionSpec as P

HEADS = 4
PER_HEAD = 8
WIDTH = 128
RESPONSE = 64
PROMPT = 1024
QUARTER = 256
ROWS = 128
KEYS = PROMPT + ROWS
STACK = 2
CHUNKS = PER_HEAD // STACK
SCALE = 1.0 / math.sqrt(WIDTH)
LOG_SCALE = SCALE * math.log2(math.e)
F32 = jnp.float32
BF16 = jnp.bfloat16
NT = (((1,), (1,)), ((), ()))
NN = (((1,), (0,)), ((), ()))
TN = (((0,), (0,)), ((), ()))


def dot(a, b, dims):
    return lax.dot_general(a, b, dims, preferred_element_type=F32)


def fill_bias(bias, me, pre_len, len0, len1):
    base = me % 4
    row = lax.broadcasted_iota(jnp.int32, (ROWS, QUARTER), 0)
    col = lax.broadcasted_iota(jnp.int32, (ROWS, QUARTER), 1)
    low, high = base % 2, base // 2
    for b, (flip_low, flip_high) in enumerate(((0, 0), (0, 1), (1, 0), (1, 1))):
        lo = 1 - low if flip_low else low
        hi = 1 - high if flip_high else high
        position = (hi * 2 + lo) * QUARTER + col
        bias[:, b * QUARTER : (b + 1) * QUARTER] = jnp.where(position < pre_len, 0.0, -1e30)
    row = lax.broadcasted_iota(jnp.int32, (ROWS, ROWS), 0)
    col = lax.broadcasted_iota(jnp.int32, (ROWS, ROWS), 1)
    first = (row < RESPONSE) & (col <= row) & (col < len0)
    second = (col >= RESPONSE) & (col <= row) & (col - RESPONSE < len1)
    bias[:, PROMPT:] = jnp.where(first | second, 0.0, -1e30)


def attend_chunk(g, chunk, q_ref, up_ref, kv, bias, live, out_ref, gq_ref, acc):
    column = g * PER_HEAD * WIDTH + chunk * STACK * WIDTH
    start = column if isinstance(column, int) else pl.multiple_of(column, STACK * WIDTH)
    q_wide = q_ref[:, pl.ds(start, STACK * WIDTH)]
    up_wide = up_ref[:, pl.ds(start, STACK * WIDTH)]
    q = jnp.concatenate([q_wide[:, i * WIDTH : (i + 1) * WIDTH] for i in range(STACK)], axis=0)
    up = jnp.concatenate([up_wide[:, i * WIDTH : (i + 1) * WIDTH] for i in range(STACK)], axis=0)
    live_rows = jnp.concatenate([live] * STACK, axis=0) > 0.5
    up = jnp.where(live_rows, up.astype(F32), 0.0).astype(BF16)
    keys = kv[g, 0]
    values = kv[g, 1]
    s = dot(q, keys, NT).reshape(STACK, ROWS, KEYS) + bias[...][None]
    s = s.reshape(STACK * ROWS, KEYS)
    top = jnp.max(s, axis=1, keepdims=True)
    e = jnp.exp2((s - top) * LOG_SCALE)
    inverse = 1.0 / jnp.sum(e, axis=1, keepdims=True)
    p = e * inverse
    weight = p.astype(BF16)
    dp = dot(up, values, NT)
    delta = jnp.sum(p * dp, axis=1, keepdims=True)
    ds = (p * (dp - delta)).astype(BF16)
    o = jnp.where(live_rows, dot(weight, values, NN), 0.0).astype(BF16)
    dq = (dot(ds, keys, NN) * SCALE).astype(BF16)
    for i in range(STACK):
        place = pl.ds(start + i * WIDTH, WIDTH)
        out_ref[:, place] = o[i * ROWS : (i + 1) * ROWS]
        gq_ref[:, place] = dq[i * ROWS : (i + 1) * ROWS]
    dk = dot(q, ds, TN)
    dv = dot(up, weight, TN)
    acc[g, 0] += dk
    acc[g, 1] += dv


def kernel(
    plen_ref, owner_ref, rprompt_ref, rlen_ref,
    q_ref, up_ref, rk_ref, rv_ref, pk_ref, pv_ref,
    out_ref, gq_ref, grk_ref, grv_ref, gpk_ref, gpv_ref,
    kv, own, zbuf, bias, live, acc, crecv, ysend, yrecv, final, zsend, zrecv,
    za, ya, ca, fa, cb, yb, zb,
):
    me = lax.axis_index("seq")
    core = me + 1 - 2 * (me % 2)
    ypart = me + 2 - 4 * (me // 2 % 2)
    zpart = me + 4 - 8 * (me // 4 % 2)

    barrier = pltpu.get_barrier_semaphore()
    for other in (core, ypart, zpart):
        pl.semaphore_signal(barrier, inc=1, device_id={"seq": other})

    for g in range(HEADS):
        columns = slice(g * WIDTH, (g + 1) * WIDTH)
        own[g, 0] = pk_ref[:, columns]
        own[g, 1] = pv_ref[:, columns]
    pl.semaphore_wait(barrier, 3)

    def send(src, dst, sems, index, other):
        copy = pltpu.make_async_remote_copy(
            src_ref=src, dst_ref=dst, send_sem=sems.at[0, index], recv_sem=sems.at[1, index],
            device_id={"seq": other},
        )
        copy.start()
        return copy

    z_in = [send(own.at[g], zbuf.at[g], za, g, zpart) for g in range(HEADS)]

    prompt = rprompt_ref[0]
    pre_len = plen_ref[prompt]
    flipped = owner_ref[prompt] != me // 4
    len0, len1 = rlen_ref[0], rlen_ref[1]
    for g in range(HEADS):
        columns = slice(g * WIDTH, (g + 1) * WIDTH)
        kv[g, 0, PROMPT:] = rk_ref[:, columns]
        kv[g, 1, PROMPT:] = rv_ref[:, columns]
    fill_bias(bias, me, pre_len, len0, len1)
    row = lax.broadcasted_iota(jnp.int32, (ROWS, WIDTH), 0)
    live[...] = jnp.where(((row < RESPONSE) & (row < len0)) | ((row >= RESPONSE) & (row - RESPONSE < len1)), 1.0, 0.0)
    acc[...] = jnp.zeros_like(acc)

    y_in, c_in, f_in = [], [], []
    c_out, y_out, z_out = [], [], []

    def gather_first(g):
        z_in[g].wait_recv()
        kv[g, :, 0:QUARTER] = jnp.where(flipped, zbuf[g], own[g])
        y_in.append(send(kv.at[g, :, 0:QUARTER], kv.at[g, :, QUARTER : 2 * QUARTER], ya, g, ypart))
        c_in.append(send(kv.at[g, :, 0:QUARTER], kv.at[g, :, 2 * QUARTER : 3 * QUARTER], ca, g, core))

    def gather_second(g):
        y_in[g].wait_recv()
        f_in.append(send(kv.at[g, :, QUARTER : 2 * QUARTER], kv.at[g, :, 3 * QUARTER : PROMPT], fa, g, core))

    def gather_last(g):
        c_in[g].wait_recv()
        f_in[g].wait_recv()

    def attend(g, low, high):
        def body(chunk, carry):
            attend_chunk(g, chunk, q_ref, up_ref, kv, bias, live[...], out_ref, gq_ref, acc)
            return carry

        lax.fori_loop(low, high, body, 0)

    def reduce_core(g):
        c_out.append(send(acc.at[g, :, :, 2 * QUARTER : PROMPT], crecv.at[g], cb, g, core))
        columns = slice(g * WIDTH, (g + 1) * WIDTH)
        grk_ref[:, columns] = (acc[g, 0, :, PROMPT:].T * SCALE).astype(BF16)
        grv_ref[:, columns] = acc[g, 1, :, PROMPT:].T.astype(BF16)

    def reduce_y(g):
        c_out[g].wait_recv()
        ysend[g] = (acc[g, :, :, QUARTER : 2 * QUARTER] + crecv[g, :, :, QUARTER:]).astype(BF16)
        y_out.append(send(ysend.at[g], yrecv.at[g], yb, g, ypart))

    def reduce_z(g):
        y_out[g].wait_recv()
        total = acc[g, :, :, 0:QUARTER] + crecv[g, :, :, 0:QUARTER] + yrecv[g].astype(F32)
        final[g] = total
        zsend[g] = total.astype(BF16)
        z_out.append(send(zsend.at[g], zrecv.at[g], zb, g, zpart))

    def finish(g):
        z_out[g].wait_recv()
        total = jnp.where(flipped, zrecv[g].astype(F32), final[g])
        columns = slice(g * WIDTH, (g + 1) * WIDTH)
        gpk_ref[:, columns] = total[0].T * SCALE
        gpv_ref[:, columns] = total[1].T

    half = CHUNKS // 2
    gather_first(0)
    gather_second(0)
    gather_first(1)
    gather_last(0)
    for g in range(HEADS):
        attend(g, 0, half)
        if g + 1 < HEADS:
            gather_second(g + 1)
        if g + 2 < HEADS:
            gather_first(g + 2)
        if g >= 1:
            reduce_y(g - 1)
        if g >= 2:
            finish(g - 2)
        attend(g, half, CHUNKS)
        if g + 1 < HEADS:
            gather_last(g + 1)
        reduce_core(g)
        if g >= 1:
            reduce_z(g - 1)
    last = HEADS - 1
    reduce_y(last)
    reduce_z(last)
    finish(last - 1)
    finish(last)
    for copy in z_in + y_in + c_in + f_in + c_out + y_out + z_out:
        copy.wait_send()


def on_device(queries, response_keys, response_values, prompt_key_rows, prompt_value_rows, upstream,
              prompt_len, prompt_owner, response_prompt, response_len):
    smem = pl.BlockSpec(memory_space=pltpu.SMEM)
    vmem = pl.BlockSpec(memory_space=pltpu.VMEM)
    shape = jax.ShapeDtypeStruct
    wide = shape(queries.shape, BF16)
    thin = shape(response_keys.shape, BF16)
    prefix = shape(prompt_key_rows.shape, F32)
    pair = pltpu.SemaphoreType.DMA((2, HEADS))
    return tuple(pl.pallas_call(
        kernel,
        out_shape=(wide, wide, thin, thin, prefix, prefix),
        in_specs=[smem] * 4 + [vmem] * 6,
        out_specs=[vmem] * 6,
        scratch_shapes=[
            pltpu.VMEM((HEADS, 2, KEYS, WIDTH), BF16),
            pltpu.VMEM((HEADS, 2, QUARTER, WIDTH), BF16),
            pltpu.VMEM((HEADS, 2, QUARTER, WIDTH), BF16),
            pltpu.VMEM((ROWS, KEYS), F32),
            pltpu.VMEM((ROWS, WIDTH), F32),
            pltpu.VMEM((HEADS, 2, WIDTH, KEYS), F32),
            pltpu.VMEM((HEADS, 2, WIDTH, 2 * QUARTER), F32),
            pltpu.VMEM((HEADS, 2, WIDTH, QUARTER), BF16),
            pltpu.VMEM((HEADS, 2, WIDTH, QUARTER), BF16),
            pltpu.VMEM((HEADS, 2, WIDTH, QUARTER), F32),
            pltpu.VMEM((HEADS, 2, WIDTH, QUARTER), BF16),
            pltpu.VMEM((HEADS, 2, WIDTH, QUARTER), BF16),
        ] + [pair] * 7,
        compiler_params=pltpu.CompilerParams(
            collective_id=0, has_side_effects=True, vmem_limit_bytes=56 * 1024 * 1024
        ),
        cost_estimate=pl.CostEstimate(flops=7 * 10**9, bytes_accessed=7 * 10**6, transcendentals=5 * 10**6),
        name="grouped",
    )(prompt_len, prompt_owner, response_prompt, response_len,
      queries, upstream, response_keys, response_values, prompt_key_rows, prompt_value_rows))


def solution(mesh):
    rows = P(("groups", "seq"), None)
    return jax.shard_map(
        on_device,
        mesh=mesh,
        in_specs=(rows,) * 6 + (P("groups"), P("groups"), P(("groups", "seq")), P(("groups", "seq"))),
        out_specs=(rows,) * 6,
        check_vma=False,
    )
```

```python
import functools
import math

import jax
import jax.numpy as jnp
from jax import lax
from jax.experimental import pallas as pl
from jax.experimental.pallas import tpu as pltpu
from jax.sharding import PartitionSpec as P

HEADS = 4
PER_HEAD = 8
WIDTH = 128
RESPONSE = 64
PROMPT = 1024
QUARTER = 256
ROWS = 128
KEYS = PROMPT + ROWS
STACK = 4
CHUNKS = PER_HEAD // STACK
SCALE = 1.0 / math.sqrt(WIDTH)
LOG_SCALE = SCALE * math.log2(math.e)
F32 = jnp.float32
BF16 = jnp.bfloat16
NT = (((1,), (1,)), ((), ()))
NN = (((1,), (0,)), ((), ()))
TN = (((0,), (0,)), ((), ()))


def dot(a, b, dims):
    return lax.dot_general(a, b, dims, preferred_element_type=F32)


def fill_bias(bias, me, pre_len, len0, len1):
    base = me % 4
    row = lax.broadcasted_iota(jnp.int32, (ROWS, QUARTER), 0)
    col = lax.broadcasted_iota(jnp.int32, (ROWS, QUARTER), 1)
    low, high = base % 2, base // 2
    for b, (flip_low, flip_high) in enumerate(((0, 0), (0, 1), (1, 0), (1, 1))):
        lo = 1 - low if flip_low else low
        hi = 1 - high if flip_high else high
        position = (hi * 2 + lo) * QUARTER + col
        bias[:, b * QUARTER : (b + 1) * QUARTER] = jnp.where(position < pre_len, 0.0, -1e30)
    row = lax.broadcasted_iota(jnp.int32, (ROWS, ROWS), 0)
    col = lax.broadcasted_iota(jnp.int32, (ROWS, ROWS), 1)
    first = (row < RESPONSE) & (col <= row) & (col < len0)
    second = (col >= RESPONSE) & (col <= row) & (col - RESPONSE < len1)
    bias[:, PROMPT:] = jnp.where(first | second, 0.0, -1e30)


def attend_chunk(g, chunk, q_ref, up_ref, kv, bias, live, out_ref, gq_ref, acc, before_values, after_values):
    start = g * PER_HEAD * WIDTH + chunk * STACK * WIDTH
    heads = [slice(start + i * WIDTH, start + (i + 1) * WIDTH) for i in range(STACK)]
    q = jnp.concatenate([q_ref[:, h] for h in heads], axis=0)
    up = jnp.concatenate([up_ref[:, h] for h in heads], axis=0)
    live_rows = jnp.concatenate([live] * STACK, axis=0) > 0.5
    up = jnp.where(live_rows, up.astype(F32), 0.0).astype(BF16)
    keys = kv[g, 0]
    s = dot(q, keys, NT).reshape(STACK, ROWS, KEYS) + bias[...][None]
    s = s.reshape(STACK * ROWS, KEYS)
    top = jnp.max(s, axis=1, keepdims=True)
    e = jnp.exp2((s - top) * LOG_SCALE)
    inverse = 1.0 / jnp.sum(e, axis=1, keepdims=True)
    p = e * inverse
    weight = p.astype(BF16)
    before_values()
    dv = dot(up, weight, TN)
    if chunk == 0:
        acc[g, 1] = dv
    else:
        acc[g, 1] += dv
    after_values()
    values = kv[g, 1]
    dp = dot(up, values, NT)
    delta = jnp.sum(p * dp, axis=1, keepdims=True)
    ds = (p * (dp - delta)).astype(BF16)
    dk = dot(q, ds, TN)
    if chunk == 0:
        acc[g, 0] = dk
    else:
        acc[g, 0] += dk
    o = jnp.where(live_rows, dot(weight, values, NN), 0.0).astype(BF16)
    dq = (dot(ds, keys, NN) * SCALE).astype(BF16)
    for i, h in enumerate(heads):
        out_ref[:, h] = o[i * ROWS : (i + 1) * ROWS]
        gq_ref[:, h] = dq[i * ROWS : (i + 1) * ROWS]


def kernel(
    plen_ref, owner_ref, rprompt_ref, rlen_ref,
    q_hbm, up_hbm, rk_ref, rv_ref, pk_ref, pv_ref,
    out_ref, gq_ref, grk_ref, grv_ref, gpk_ref, gpv_ref,
    q_ref, up_ref, kv, zbuf, bias, live, acc, crecv, ysend, yrecv, final, zsend, zrecv,
    za, ya, ca, fa, cb, yb, zb, local,
):
    me = lax.axis_index("seq")
    core = me + 1 - 2 * (me % 2)
    ypart = me + 2 - 4 * (me // 2 % 2)
    zpart = me + 4 - 8 * (me // 4 % 2)
    prompt_refs = (pk_ref, pv_ref)
    response_refs = (rk_ref, rv_ref)

    barrier = pltpu.get_barrier_semaphore()
    for other in (zpart, ypart, core):
        pl.semaphore_signal(barrier, inc=1, device_id={"seq": other})
    loads = [
        pltpu.make_async_copy(q_hbm, q_ref, local.at[0]),
        pltpu.make_async_copy(up_hbm, up_ref, local.at[1]),
    ]
    for load in loads:
        load.start()
    pl.semaphore_wait(barrier, 3)

    def columns(g):
        return slice(g * WIDTH, (g + 1) * WIDTH)

    def send(src, dst, sems, g, k, other):
        copy = pltpu.make_async_remote_copy(
            src_ref=src, dst_ref=dst, send_sem=sems.at[0, 2 * g + k], recv_sem=sems.at[1, 2 * g + k],
            device_id={"seq": other},
        )
        copy.start()
        return copy

    z_in, y_in, c_in, f_in, c_out, y_out, z_out = ({} for _ in range(7))
    for g in range(HEADS):
        for k in range(2):
            z_in[g, k] = send(prompt_refs[k].at[:, columns(g)], zbuf.at[g, k], za, g, k, zpart)

    prompt = rprompt_ref[0]
    pre_len = plen_ref[prompt]
    flipped = owner_ref[prompt] != me // 4
    len0, len1 = rlen_ref[0], rlen_ref[1]
    for g in range(HEADS):
        for k in range(2):
            kv[g, k, PROMPT:] = response_refs[k][:, columns(g)]
    fill_bias(bias, me, pre_len, len0, len1)
    row = lax.broadcasted_iota(jnp.int32, (ROWS, WIDTH), 0)
    live[...] = jnp.where(((row < RESPONSE) & (row < len0)) | ((row >= RESPONSE) & (row - RESPONSE < len1)), 1.0, 0.0)

    def gather_first(g, k):
        z_in[g, k].wait_recv()
        kv[g, k, 0:QUARTER] = jnp.where(flipped, zbuf[g, k], prompt_refs[k][:, columns(g)])
        mine = kv.at[g, k, 0:QUARTER]
        y_in[g, k] = send(mine, kv.at[g, k, QUARTER : 2 * QUARTER], ya, g, k, ypart)
        c_in[g, k] = send(mine, kv.at[g, k, 2 * QUARTER : 3 * QUARTER], ca, g, k, core)

    def gather_second(g, k):
        y_in[g, k].wait_recv()
        f_in[g, k] = send(kv.at[g, k, QUARTER : 2 * QUARTER], kv.at[g, k, 3 * QUARTER : PROMPT], fa, g, k, core)

    def gather_last(g, k):
        c_in[g, k].wait_recv()
        f_in[g, k].wait_recv()

    def reduce_core(g, k):
        c_out[g, k] = send(acc.at[g, k, :, 2 * QUARTER : PROMPT], crecv.at[g, k], cb, g, k, core)

    def own_grads(g):
        grk_ref[:, columns(g)] = (acc[g, 0, :, PROMPT:].T * SCALE).astype(BF16)
        grv_ref[:, columns(g)] = acc[g, 1, :, PROMPT:].T.astype(BF16)

    def reduce_y(g, k):
        c_out[g, k].wait_recv()
        ysend[g, k] = (acc[g, k, :, QUARTER : 2 * QUARTER] + crecv[g, k, :, QUARTER:]).astype(BF16)
        y_out[g, k] = send(ysend.at[g, k], yrecv.at[g, k], yb, g, k, ypart)

    def reduce_z(g, k):
        y_out[g, k].wait_recv()
        total = acc[g, k, :, 0:QUARTER] + crecv[g, k, :, 0:QUARTER] + yrecv[g, k].astype(F32)
        final[g, k] = total
        zsend[g, k] = total.astype(BF16)
        z_out[g, k] = send(zsend.at[g, k], zrecv.at[g, k], zb, g, k, zpart)

    def finish(g, k):
        z_out[g, k].wait_recv()
        total = jnp.where(flipped, zrecv[g, k].astype(F32), final[g, k])
        if k == 0:
            gpk_ref[:, columns(g)] = total.T * SCALE
        else:
            gpv_ref[:, columns(g)] = total.T

    def both(step, g):
        for k in (1, 0):
            step(g, k)

    def nothing():
        pass

    def attend(g, chunk, before=nothing, after=nothing):
        attend_chunk(g, chunk, q_ref, up_ref, kv, bias, live[...], out_ref, gq_ref, acc, before, after)

    last = HEADS - 1
    gather_first(0, 0)
    gather_first(0, 1)
    gather_second(0, 0)
    gather_first(1, 0)
    gather_second(0, 1)
    gather_first(1, 1)
    for load in loads:
        load.wait()
    gather_last(0, 0)
    for g in range(HEADS):
        attend(g, 0, before=functools.partial(gather_last, g, 1) if g == 0 else nothing)
        if g == 0:
            both(gather_second, 1)
            both(gather_first, 2)
        elif g + 1 < HEADS:
            both(gather_second, g + 1)
        if g >= 1:
            both(reduce_y, g - 1)
        if g >= 2:
            both(reduce_z, g - 2)
        if g >= 3:
            both(finish, g - 3)
        attend(g, 1, after=functools.partial(reduce_core, g, 1))
        reduce_core(g, 0)
        if g == last:
            reduce_y(g, 1)
            reduce_y(g, 0)
        own_grads(g)
        if g + 1 < HEADS:
            both(gather_last, g + 1)
        if g + 3 < HEADS:
            both(gather_first, g + 3)
    both(reduce_z, last - 1)
    both(finish, last - 2)
    both(reduce_z, last)
    both(finish, last - 1)
    both(finish, last)
    for group in (z_in, y_in, c_in, f_in, c_out, y_out, z_out):
        for copy in group.values():
            copy.wait_send()


def on_device(queries, response_keys, response_values, prompt_key_rows, prompt_value_rows, upstream,
              prompt_len, prompt_owner, response_prompt, response_len):
    smem = pl.BlockSpec(memory_space=pltpu.SMEM)
    vmem = pl.BlockSpec(memory_space=pltpu.VMEM)
    shape = jax.ShapeDtypeStruct
    wide = shape(queries.shape, BF16)
    thin = shape(response_keys.shape, BF16)
    prefix = shape(prompt_key_rows.shape, F32)
    pair = pltpu.SemaphoreType.DMA((2, 2 * HEADS))
    return tuple(pl.pallas_call(
        kernel,
        out_shape=tuple(pltpu.VMEM(o.shape, o.dtype) for o in (wide, wide, thin, thin, prefix, prefix)),
        in_specs=[smem] * 4 + [pl.BlockSpec(memory_space=pl.ANY)] * 2 + [vmem] * 4,
        out_specs=[vmem] * 6,
        scratch_shapes=[
            pltpu.VMEM(queries.shape, BF16),
            pltpu.VMEM(queries.shape, BF16),
            pltpu.VMEM((HEADS, 2, KEYS, WIDTH), BF16),
            pltpu.VMEM((HEADS, 2, QUARTER, WIDTH), BF16),
            pltpu.VMEM((ROWS, KEYS), F32),
            pltpu.VMEM((ROWS, WIDTH), F32),
            pltpu.VMEM((HEADS, 2, WIDTH, KEYS), F32),
            pltpu.VMEM((HEADS, 2, WIDTH, 2 * QUARTER), F32),
            pltpu.VMEM((HEADS, 2, WIDTH, QUARTER), BF16),
            pltpu.VMEM((HEADS, 2, WIDTH, QUARTER), BF16),
            pltpu.VMEM((HEADS, 2, WIDTH, QUARTER), F32),
            pltpu.VMEM((HEADS, 2, WIDTH, QUARTER), BF16),
            pltpu.VMEM((HEADS, 2, WIDTH, QUARTER), BF16),
        ] + [pair] * 7 + [pltpu.SemaphoreType.DMA((2,))],
        compiler_params=pltpu.CompilerParams(
            collective_id=0, has_side_effects=True, vmem_limit_bytes=56 * 1024 * 1024
        ),
        cost_estimate=pl.CostEstimate(flops=7 * 10**9, bytes_accessed=7 * 10**6, transcendentals=5 * 10**6),
        name="grouped",
    )(prompt_len, prompt_owner, response_prompt, response_len,
      queries, upstream, response_keys, response_values, prompt_key_rows, prompt_value_rows))


def solution(mesh):
    rows = P(("groups", "seq"), None)
    return jax.shard_map(
        on_device,
        mesh=mesh,
        in_specs=(rows,) * 6 + (P("groups"), P("groups"), P(("groups", "seq")), P(("groups", "seq"))),
        out_specs=(rows,) * 6,
        check_vma=False,
    )
```

```python
import functools
import math

import jax
import jax.numpy as jnp
from jax import lax
from jax.experimental import pallas as pl
from jax.experimental.pallas import tpu as pltpu
from jax.sharding import PartitionSpec as P

HEADS = 4
PER_HEAD = 8
WIDTH = 128
RESPONSE = 64
PROMPT = 1024
QUARTER = 256
ROWS = 128
KEYS = PROMPT + ROWS
STACK = 4
CHUNKS = PER_HEAD // STACK
SCALE = 1.0 / math.sqrt(WIDTH)
LOG_SCALE = SCALE * math.log2(math.e)
F32 = jnp.float32
BF16 = jnp.bfloat16
NT = (((1,), (1,)), ((), ()))
NN = (((1,), (0,)), ((), ()))
TN = (((0,), (0,)), ((), ()))


def dot(a, b, dims):
    return lax.dot_general(a, b, dims, preferred_element_type=F32)


def fill_bias(bias, me, pre_len, len0, len1):
    base = me % 4
    row = lax.broadcasted_iota(jnp.int32, (ROWS, QUARTER), 0)
    col = lax.broadcasted_iota(jnp.int32, (ROWS, QUARTER), 1)
    low, high = base % 2, base // 2
    for b, (flip_low, flip_high) in enumerate(((0, 0), (0, 1), (1, 0), (1, 1))):
        lo = 1 - low if flip_low else low
        hi = 1 - high if flip_high else high
        position = (hi * 2 + lo) * QUARTER + col
        bias[:, b * QUARTER : (b + 1) * QUARTER] = jnp.where(position < pre_len, 0.0, -1e30)
    row = lax.broadcasted_iota(jnp.int32, (ROWS, ROWS), 0)
    col = lax.broadcasted_iota(jnp.int32, (ROWS, ROWS), 1)
    first = (row < RESPONSE) & (col <= row) & (col < len0)
    second = (col >= RESPONSE) & (col <= row) & (col - RESPONSE < len1)
    bias[:, PROMPT:] = jnp.where(first | second, 0.0, -1e30)


def attend_chunk(g, chunk, q_ref, up_ref, kv, bias, live, out_ref, gq_ref, acc, before_values, after_values, after_keys):
    start = g * PER_HEAD * WIDTH + chunk * STACK * WIDTH
    heads = [slice(start + i * WIDTH, start + (i + 1) * WIDTH) for i in range(STACK)]
    q = jnp.concatenate([q_ref[:, h] for h in heads], axis=0)
    up = jnp.concatenate([up_ref[:, h] for h in heads], axis=0)
    live_rows = jnp.concatenate([live] * STACK, axis=0) > 0.5
    up = jnp.where(live_rows, up.astype(F32), 0.0).astype(BF16)
    keys = kv[g, 0]
    s = dot(q, keys, NT).reshape(STACK, ROWS, KEYS) + bias[...][None]
    s = s.reshape(STACK * ROWS, KEYS)
    top = jnp.max(s, axis=1, keepdims=True)
    e = jnp.exp2((s - top) * LOG_SCALE)
    inverse = 1.0 / jnp.sum(e, axis=1, keepdims=True)
    p = e * inverse
    weight = p.astype(BF16)
    before_values()
    dv = dot(up, weight, TN)
    if chunk == 0:
        acc[g, 1] = dv
    else:
        acc[g, 1] += dv
    after_values()
    values = kv[g, 1]
    dp = dot(up, values, NT)
    delta = jnp.sum(p * dp, axis=1, keepdims=True)
    ds = (p * (dp - delta)).astype(BF16)
    dk = dot(q, ds, TN)
    if chunk == 0:
        acc[g, 0] = dk
    else:
        acc[g, 0] += dk
    after_keys()
    o = jnp.where(live_rows, dot(weight, values, NN), 0.0).astype(BF16)
    dq = (dot(ds, keys, NN) * SCALE).astype(BF16)
    for i, h in enumerate(heads):
        out_ref[:, h] = o[i * ROWS : (i + 1) * ROWS]
        gq_ref[:, h] = dq[i * ROWS : (i + 1) * ROWS]


def kernel(
    plen_ref, owner_ref, rprompt_ref, rlen_ref,
    q_hbm, up_hbm, rk_ref, rv_ref, pk_ref, pv_ref,
    out_ref, gq_ref, grk_ref, grv_ref, gpk_ref, gpv_ref,
    q_ref, up_ref, kv, zbuf, bias, live, acc, crecv, ysend, yrecv, final, zsend, zrecv,
    za, ya, ca, fa, cb, yb, zb, local,
):
    me = lax.axis_index("seq")
    core = me + 1 - 2 * (me % 2)
    ypart = me + 2 - 4 * (me // 2 % 2)
    zpart = me + 4 - 8 * (me // 4 % 2)
    prompt_refs = (pk_ref, pv_ref)
    response_refs = (rk_ref, rv_ref)

    barrier = pltpu.get_barrier_semaphore()
    for other in (zpart, ypart, core):
        pl.semaphore_signal(barrier, inc=1, device_id={"seq": other})
    loads = [
        pltpu.make_async_copy(q_hbm, q_ref, local.at[0]),
        pltpu.make_async_copy(up_hbm, up_ref, local.at[1]),
    ]
    for load in loads:
        load.start()
    pl.semaphore_wait(barrier, 3)

    def columns(g):
        return slice(g * WIDTH, (g + 1) * WIDTH)

    def send(src, dst, sems, g, k, other):
        copy = pltpu.make_async_remote_copy(
            src_ref=src, dst_ref=dst, send_sem=sems.at[0, 2 * g + k], recv_sem=sems.at[1, 2 * g + k],
            device_id={"seq": other},
        )
        copy.start()
        return copy

    z_in, y_in, c_in, f_in, c_out, y_out, z_out = ({} for _ in range(7))
    for g in range(HEADS):
        for k in range(2):
            z_in[g, k] = send(prompt_refs[k].at[:, columns(g)], zbuf.at[g, k], za, g, k, zpart)

    prompt = rprompt_ref[0]
    pre_len = plen_ref[prompt]
    flipped = owner_ref[prompt] != me // 4
    len0, len1 = rlen_ref[0], rlen_ref[1]
    for g in range(HEADS):
        for k in range(2):
            kv[g, k, PROMPT:] = response_refs[k][:, columns(g)]
    fill_bias(bias, me, pre_len, len0, len1)
    row = lax.broadcasted_iota(jnp.int32, (ROWS, WIDTH), 0)
    live[...] = jnp.where(((row < RESPONSE) & (row < len0)) | ((row >= RESPONSE) & (row - RESPONSE < len1)), 1.0, 0.0)

    def gather_first(g, k):
        z_in[g, k].wait_recv()
        kv[g, k, 0:QUARTER] = jnp.where(flipped, zbuf[g, k], prompt_refs[k][:, columns(g)])
        mine = kv.at[g, k, 0:QUARTER]
        y_in[g, k] = send(mine, kv.at[g, k, QUARTER : 2 * QUARTER], ya, g, k, ypart)
        c_in[g, k] = send(mine, kv.at[g, k, 2 * QUARTER : 3 * QUARTER], ca, g, k, core)

    def gather_second(g, k):
        y_in[g, k].wait_recv()
        f_in[g, k] = send(kv.at[g, k, QUARTER : 2 * QUARTER], kv.at[g, k, 3 * QUARTER : PROMPT], fa, g, k, core)

    def gather_last(g, k):
        c_in[g, k].wait_recv()
        f_in[g, k].wait_recv()

    def reduce_core(g, k):
        c_out[g, k] = send(acc.at[g, k, :, 2 * QUARTER : PROMPT], crecv.at[g, k], cb, g, k, core)

    def own_grads(g):
        grk_ref[:, columns(g)] = (acc[g, 0, :, PROMPT:].T * SCALE).astype(BF16)
        grv_ref[:, columns(g)] = acc[g, 1, :, PROMPT:].T.astype(BF16)

    def reduce_y(g, k):
        c_out[g, k].wait_recv()
        ysend[g, k] = (acc[g, k, :, QUARTER : 2 * QUARTER] + crecv[g, k, :, QUARTER:]).astype(BF16)
        y_out[g, k] = send(ysend.at[g, k], yrecv.at[g, k], yb, g, k, ypart)

    def reduce_z(g, k):
        y_out[g, k].wait_recv()
        total = acc[g, k, :, 0:QUARTER] + crecv[g, k, :, 0:QUARTER] + yrecv[g, k].astype(F32)
        final[g, k] = total
        zsend[g, k] = total.astype(BF16)
        z_out[g, k] = send(zsend.at[g, k], zrecv.at[g, k], zb, g, k, zpart)

    def finish(g, k):
        z_out[g, k].wait_recv()
        total = jnp.where(flipped, zrecv[g, k].astype(F32), final[g, k])
        if k == 0:
            gpk_ref[:, columns(g)] = total.T * SCALE
        else:
            gpv_ref[:, columns(g)] = total.T

    def both(step, g):
        for k in (1, 0):
            step(g, k)

    def nothing():
        pass

    def attend(g, chunk, before=nothing, after=nothing, keyed=nothing):
        attend_chunk(g, chunk, q_ref, up_ref, kv, bias, live[...], out_ref, gq_ref, acc, before, after, keyed)

    last = HEADS - 1

    def after_key(g):
        reduce_core(g, 0)
        if g == last:
            reduce_y(g, 1)

    gather_first(0, 0)
    gather_first(0, 1)
    gather_second(0, 0)
    gather_first(1, 0)
    gather_second(0, 1)
    gather_first(1, 1)
    for load in loads:
        load.wait()
    gather_last(0, 0)
    for g in range(HEADS):
        attend(g, 0, before=functools.partial(gather_last, g, 1) if g == 0 else nothing)
        if g == 0:
            both(gather_second, 1)
            both(gather_first, 2)
        elif g + 1 < HEADS:
            both(gather_second, g + 1)
        if g >= 1:
            both(reduce_y, g - 1)
        if g >= 2:
            both(reduce_z, g - 2)
        if g >= 3:
            both(finish, g - 3)
        attend(g, 1, nothing, functools.partial(reduce_core, g, 1), functools.partial(after_key, g))
        if g == last:
            reduce_y(g, 0)
        own_grads(g)
        if g + 1 < HEADS:
            both(gather_last, g + 1)
        if g + 3 < HEADS:
            both(gather_first, g + 3)
    both(reduce_z, last - 1)
    both(finish, last - 2)
    both(reduce_z, last)
    both(finish, last - 1)
    both(finish, last)
    for group in (z_in, y_in, c_in, f_in, c_out, y_out, z_out):
        for copy in group.values():
            copy.wait_send()


def on_device(queries, response_keys, response_values, prompt_key_rows, prompt_value_rows, upstream,
              prompt_len, prompt_owner, response_prompt, response_len):
    smem = pl.BlockSpec(memory_space=pltpu.SMEM)
    vmem = pl.BlockSpec(memory_space=pltpu.VMEM)
    shape = jax.ShapeDtypeStruct
    wide = shape(queries.shape, BF16)
    thin = shape(response_keys.shape, BF16)
    prefix = shape(prompt_key_rows.shape, F32)
    pair = pltpu.SemaphoreType.DMA((2, 2 * HEADS))
    return tuple(pl.pallas_call(
        kernel,
        out_shape=tuple(pltpu.VMEM(o.shape, o.dtype) for o in (wide, wide, thin, thin, prefix, prefix)),
        in_specs=[smem] * 4 + [pl.BlockSpec(memory_space=pl.ANY)] * 2 + [vmem] * 4,
        out_specs=[vmem] * 6,
        scratch_shapes=[
            pltpu.VMEM(queries.shape, BF16),
            pltpu.VMEM(queries.shape, BF16),
            pltpu.VMEM((HEADS, 2, KEYS, WIDTH), BF16),
            pltpu.VMEM((HEADS, 2, QUARTER, WIDTH), BF16),
            pltpu.VMEM((ROWS, KEYS), F32),
            pltpu.VMEM((ROWS, WIDTH), F32),
            pltpu.VMEM((HEADS, 2, WIDTH, KEYS), F32),
            pltpu.VMEM((HEADS, 2, WIDTH, 2 * QUARTER), F32),
            pltpu.VMEM((HEADS, 2, WIDTH, QUARTER), BF16),
            pltpu.VMEM((HEADS, 2, WIDTH, QUARTER), BF16),
            pltpu.VMEM((HEADS, 2, WIDTH, QUARTER), F32),
            pltpu.VMEM((HEADS, 2, WIDTH, QUARTER), BF16),
            pltpu.VMEM((HEADS, 2, WIDTH, QUARTER), BF16),
        ] + [pair] * 7 + [pltpu.SemaphoreType.DMA((2,))],
        compiler_params=pltpu.CompilerParams(
            collective_id=0, has_side_effects=True, vmem_limit_bytes=56 * 1024 * 1024
        ),
        cost_estimate=pl.CostEstimate(flops=7 * 10**9, bytes_accessed=7 * 10**6, transcendentals=5 * 10**6),
        name="grouped",
    )(prompt_len, prompt_owner, response_prompt, response_len,
      queries, upstream, response_keys, response_values, prompt_key_rows, prompt_value_rows))


def solution(mesh):
    rows = P(("groups", "seq"), None)
    return jax.shard_map(
        on_device,
        mesh=mesh,
        in_specs=(rows,) * 6 + (P("groups"), P("groups"), P(("groups", "seq")), P(("groups", "seq"))),
        out_specs=(rows,) * 6,
        check_vma=False,
    )
```
